32 devices in a mesh: pre: 4 (over y, x), req: 4 (over z), hd: 2 (over core).
Axes of the slice: x: 2, y: 2, z: 4, core: 2. Of those that a mesh axis runs over, the one named last changes fastest.
Arguments:
- hidden: bfloat16 [8, 8192], P(None, 'req'), may hold values from -6 to 6
- gain: float32 [8192], P('req'), may hold values from 0.25 to 1.75
- w_qkv: bfloat16 [8192, 10240], P('req', ('pre', 'hd')), may hold values from -0.125 to 0.125
- w_out: bfloat16 [8192, 8192], P(('pre', 'hd'), 'req'), may hold values from -0.0625 to 0.0625
- k_pool: bfloat16 [512, 8, 64, 128], P('req', ('pre', 'hd')), may hold values from -64 to 64
- v_pool: bfloat16 [512, 8, 64, 128], P('req', ('pre', 'hd')), may hold values from -28 to 28
- block_table: int32 [8, 64], replicated, may hold values from 0 to 511, as said below
- lengths: int32 [8], replicated, may hold values from 1024 to 4096
Outputs:
- residual_out: bfloat16 [8, 8192], P(None, 'req')
- keys_out: bfloat16 [8, 8, 4096, 128], P('req', 'hd', 'pre')
- values_out: bfloat16 [8, 8, 4096, 128], P('req', 'hd', 'pre')
The draws below stay inside these ranges and needn't reach their ends.
Inputs may be any that keep to these rules, and one draw needn't show every extreme that they name: `block_table`: every pool page is named once. The pages that requests i * 2 to i * 2 + 1 hold at logical positions j * 16 to j * 16 + 15 lie exactly 8 in each block of 128 consecutive pool pages.
All inputs are finite; a program needn't handle non-finite values.
Results may differ from the reference program's by a relative error of at most 0.02.
The reference program's roundings to bfloat16 on the way count: a program that leaves them out, or rounds other values in their place, can miss the bound.
Values may be sent and summed in bfloat16 or wider, within the bound.
No kernel may reach another device: no remote copies, remote signals or barrier semaphores. Data moves between devices by JAX's collectives and lax.ppermute only.
A program may use at most 64 MiB of HBM per device.

```python
import math
import jax
import jax.numpy as jnp
from jax import lax

D = 8192
HQ = 64
KVH = 8
HD = 128
PAGE = 64
PPR = 64
STEPS = 2
REQ_DEV = 2
R = 8
POOL = 512
PAGES_DEV = 128
PART = 16
PAIR = 8
CTX = 4096
N_PRE = 4
N_REQ = 4
N_HD = 2


def draw_k_pool(key, part):
    key = jax.random.fold_in(key, 11)
    scale_key, entry_key = jax.random.split(key, 2)
    target_shape = (POOL, KVH, PAGE, HD)
    page_scale = jnp.exp(jax.random.uniform(scale_key, (POOL, KVH, 1, 1), minval=math.log(0.5), maxval=math.log(2.0)))
    result = jnp.clip(jax.random.normal(entry_key, target_shape), -6.0, 6.0) * page_scale
    return result.astype(jnp.bfloat16)


def draw_v_pool(key, part):
    key = jax.random.fold_in(key, 23)
    scale_key, entry_key = jax.random.split(key)
    target_shape = (POOL, KVH, PAGE, HD)
    page_scale = jnp.exp(jax.random.uniform(scale_key, (POOL, KVH, 1, 1), minval=math.log(0.5), maxval=math.log(2.0)))
    entries = jnp.clip(jax.random.normal(entry_key, target_shape), -6.0, 6.0)
    return (entries * page_scale).astype(jnp.bfloat16)


def draw_block_table(key, part):
    key = jax.random.fold_in(key, 37)
    dest_key, group_key = jax.random.split(key)
    dest_count = N_PRE * N_REQ
    local_pages = REQ_DEV * PART
    dest_perms = jax.vmap(lambda single: jax.random.permutation(single, local_pages))(jax.random.split(dest_key, dest_count))
    group_perms = jax.vmap(lambda single: jax.random.permutation(single, PAGES_DEV))(jax.random.split(group_key, N_REQ))
    source_group = dest_perms // PAIR
    within = dest_perms % PAIR
    dest_ids = jnp.arange(dest_count, dtype=jnp.int32)[:, None]
    slot_ids = group_perms[source_group, dest_ids * PAIR + within]
    pool_ids = source_group * PAGES_DEV + slot_ids
    pool_ids = pool_ids.reshape(N_PRE, N_REQ, REQ_DEV, PART).transpose(1, 2, 0, 3)
    return pool_ids.reshape(R, PPR).astype(jnp.int32)


def draw_lengths(key, part):
    key = jax.random.fold_in(key, 53)
    value_key, index_key = jax.random.split(key)
    values = jax.random.randint(value_key, (R,), CTX // 4, CTX + 1)
    where_max = jax.random.randint(index_key, (), 0, R)
    values = values.at[where_max].set(CTX)
    values = values.at[(where_max + 1) % R].set(CTX // 4)
    return values.astype(jnp.int32)


def levels(key, shape, pieces, least, top_value):
    level = 1.0
    for position, shards_of in pieces:
        draws = jax.random.uniform(jax.random.fold_in(jax.random.fold_in(key, 6), position), (shards_of,), jnp.float32, least / len(pieces), top_value / len(pieces))
        level = level * jnp.repeat(jnp.exp(draws), shape[position] // shards_of).reshape((-1,) + (1,) * (len(shape) - 1 - position))
    return level


def scatter_about(own_key, extent, spread, bound, shards=(), kind=jnp.bfloat16):
    array = spread * jax.random.normal(own_key, extent, jnp.float32)
    if shards:
        array = array * levels(own_key, extent, shards, -0.22, 0.18)
    return jnp.clip(array, -bound, bound).astype(kind)


def setup_inputs(seed: int = 0) -> dict:
    streams_of = jax.random.split(jax.random.key(seed), 9)
    hidden = scatter_about(streams_of[0], (R, D), 1.0, 6.0, ((1, 4),))
    gain = jnp.clip(1.0 + 0.15 * jax.random.normal(streams_of[1], (D,), jnp.float32), 0.25, 1.75)
    w_qkv = scatter_about(streams_of[2], (D, KVH * (HQ // KVH + 2) * HD), (D // 4) ** -0.5, 0.125, ((0, 4), (1, 8)))
    w_out = scatter_about(streams_of[3], (HQ * HD, D), (HQ * HD) ** -0.5, 0.0625, ((0, 8), (1, 4)))
    k_pool = draw_k_pool(jax.random.fold_in(streams_of[8], 71), 0)
    v_pool = draw_v_pool(jax.random.fold_in(streams_of[8], 71), 0)
    block_table = draw_block_table(jax.random.fold_in(streams_of[8], 71), 0)
    lengths = draw_lengths(jax.random.fold_in(streams_of[8], 71), 0)
    return dict(hidden=hidden, gain=gain, w_qkv=w_qkv, w_out=w_out, k_pool=k_pool, v_pool=v_pool, block_table=block_table, lengths=lengths)


epsilon = 1e-05
rope_theta = 500000.0

def rotate(values, positions):
    half_dim = values.shape[-1] // 2
    frequency = rope_theta ** (-jnp.arange(half_dim, dtype=jnp.float32) * 2.0 / values.shape[-1])
    angles = positions[:, None] * frequency[None, :]
    target_shape = (values.shape[0],) + (1,) * (values.ndim - 2) + (half_dim,)
    cosine = jnp.cos(angles).reshape(target_shape)
    sine_part = jnp.sin(angles).reshape(target_shape)
    first_half = values[..., :half_dim].astype(jnp.float32)
    second_half = values[..., half_dim:].astype(jnp.float32)
    return jnp.concatenate([first_half * cosine - second_half * sine_part, second_half * cosine + first_half * sine_part], -1)

def attend(row_inputs):
    query_row, keys_row, values_row, fresh_k, fresh_v, row_length = row_inputs
    score_scale = 1.0 / math.sqrt(HD)
    cached = jnp.einsum('hgd,htd->hgt', query_row.astype(jnp.float32), keys_row.astype(jnp.float32), precision=lax.Precision.HIGHEST) * score_scale
    alive_mask = jnp.arange(keys_row.shape[1]) < row_length
    cached = jnp.where(alive_mask[None, None, :], cached, -jnp.inf)
    fresh = jnp.einsum('hgd,hnd->hgn', query_row.astype(jnp.float32), fresh_k.astype(jnp.float32), precision=lax.Precision.HIGHEST) * score_scale
    weights = jax.nn.softmax(jnp.concatenate([cached, fresh], -1), axis=-1)
    values_all = jnp.concatenate([values_row.astype(jnp.float32), fresh_v.astype(jnp.float32)], axis=1)
    return jnp.einsum('hgt,htd->hgd', weights, values_all, precision=lax.Precision.HIGHEST)

def reference(hidden, gain, w_qkv, w_out, k_pool, v_pool, block_table, lengths):
    head_order = jnp.arange(KVH).reshape(N_PRE, N_HD).T.reshape(-1)
    keys_full = k_pool[block_table].transpose(0, 2, 1, 3, 4).reshape(R, KVH, PPR * PAGE, HD)
    values_full = v_pool[block_table].transpose(0, 2, 1, 3, 4).reshape(R, KVH, PPR * PAGE, HD)
    group_q = HQ // KVH
    residual_rows = hidden
    fresh_keys = []
    fresh_values = []
    for step_index in range(STEPS):
        widened = residual_rows.astype(jnp.float32)
        normed = (widened * lax.rsqrt(lax.optimization_barrier(jnp.mean(widened * widened, axis=1, keepdims=True)) + epsilon) * gain[None, :]).astype(jnp.bfloat16)
        projected = jnp.dot(normed, w_qkv, preferred_element_type=jnp.float32).astype(jnp.bfloat16)
        projected = projected.reshape(R, KVH, group_q + 2, HD)
        positions = (lengths + step_index).astype(jnp.float32)
        queries = rotate(projected[:, :, :group_q], positions).astype(jnp.bfloat16)
        fresh_keys.append(rotate(projected[:, :, group_q], positions).astype(jnp.bfloat16))
        fresh_values.append(projected[:, :, group_q + 1])
        stacked_k = jnp.stack(fresh_keys, 2)
        stacked_v = jnp.stack(fresh_values, 2)
        attended = lax.map(attend, (queries, keys_full, values_full, stacked_k, stacked_v, lengths))
        attended = attended.astype(jnp.bfloat16).reshape(R, HQ * HD)
        attn_branch = jnp.dot(attended, w_out, preferred_element_type=jnp.float32)
        residual_rows = (widened + attn_branch).astype(jnp.bfloat16)
    return (residual_rows, keys_full[:, head_order], values_full[:, head_order])
```

```python
import functools
import math

import jax
import jax.numpy as jnp
from jax import lax
from jax.experimental import pallas as pl
from jax.experimental.pallas import tpu as pltpu
from jax.sharding import PartitionSpec as P

D = 8192
STEPS = 2

epsilon = 1e-05
rope_theta = 500000.0
NEG = -1e30
F32 = jnp.float32
BF16 = jnp.bfloat16
ANY = pl.BlockSpec(memory_space=pl.ANY)
SMEM = pl.BlockSpec(memory_space=pltpu.SMEM)
VMEM = pl.BlockSpec(memory_space=pltpu.VMEM)
HBM = pl.BlockSpec(memory_space=pltpu.HBM)


def peers(value, axis):
    n = lax.axis_size(axis)
    return [value] + [
        lax.ppermute(value, axis, [(i, i ^ s) for i in range(n)]) for s in range(1, n)
    ]


def small(axis):
    n = lax.axis_size(axis)
    return n <= 4 and n & (n - 1) == 0


def tree_sum(parts):
    while len(parts) > 1:
        parts = [parts[i] + parts[i + 1] for i in range(0, len(parts), 2)]
    return parts[0]


def terms_over(value, axis):
    return peers(value, axis) if small(axis) else [lax.psum(value, axis)]


def split_rows(value):
    high = value.astype(BF16)
    low = (value - high.astype(F32)).astype(BF16)
    return jnp.concatenate([high, low])


def join_rows(both):
    rows = both.shape[0] // 2
    return both[:rows] + both[rows:]


def dot(a, b, contract=((1,), (0,))):
    return lax.dot_general(a, b, (contract, ((), ())), preferred_element_type=F32)


def pack(pools, table, ids, spec, n_req, pair):
    n = len(spec)

    def kernel(table_ref, ids_ref, k_ref, v_ref, *refs):
        outs, (held, sems) = refs[:n], refs[n:]
        copies = []
        for c, (out, (dj, dr)) in enumerate(zip(outs, spec)):
            first = ((ids_ref[0] ^ dj) * n_req + (ids_ref[1] ^ dr)) * pair
            for k in range(pair):
                slot = table_ref[first + k]
                held[c, 0, k] = k_ref[slot]
                held[c, 1, k] = v_ref[slot]
            copies.append(pltpu.make_async_copy(held.at[c], out, sems.at[c]))
            copies[-1].start()
        for copy in copies:
            copy.wait()

    piece = (2, pair, *pools[0].shape[1:])
    return pl.pallas_call(
        kernel,
        in_specs=[SMEM, SMEM, VMEM, VMEM],
        out_specs=[HBM] * n,
        out_shape=[jax.ShapeDtypeStruct(piece, BF16)] * n,
        scratch_shapes=[pltpu.VMEM((n, *piece), BF16), pltpu.SemaphoreType.DMA((n,))],
        compiler_params=pltpu.CompilerParams(vmem_limit_bytes=16 * 1024 * 1024),
        cost_estimate=pl.CostEstimate(flops=0, bytes_accessed=1024, transcendentals=0),
    )(table, ids, *pools)


def after(values, others):
    n = len(values)
    return pl.pallas_call(
        lambda *refs: None,
        in_specs=[HBM] * n + [ANY] * len(others),
        out_specs=[HBM] * n,
        out_shape=[jax.ShapeDtypeStruct(v.shape, v.dtype) for v in values],
        input_output_aliases={i: i for i in range(n)},
        compiler_params=pltpu.CompilerParams(vmem_limit_bytes=1024 * 1024),
        cost_estimate=pl.CostEstimate(flops=0, bytes_accessed=1024, transcendentals=0),
    )(*values, *others)


def call(kernel, operands, in_specs, out_shapes, out_specs, grid, scratch, cost, vmem=12):
    return pl.pallas_call(
        kernel,
        grid=grid,
        in_specs=in_specs,
        out_specs=out_specs,
        out_shape=out_shapes,
        scratch_shapes=scratch,
        compiler_params=pltpu.CompilerParams(vmem_limit_bytes=vmem * 1024 * 1024),
        cost_estimate=pl.CostEstimate(flops=0, bytes_accessed=1024, transcendentals=0),
    )(*operands)


def project(x, parts, gain, w, waits):
    rows, depth = x.shape
    cols = w.shape[1]
    block = math.gcd(depth, 512)
    lanes = 128
    n = len(parts)

    def kernel(*refs):
        x_ref, gain_ref, w_ref = refs[:3]
        part_refs = refs[3 : 3 + n]
        out_ref, new_ref = refs[-2:]
        value = x_ref[...].astype(F32)
        if n:
            value = value + tree_sum([r[...] for r in part_refs])
        new_ref[...] = value
        raw = join_rows(dot(split_rows(value * gain_ref[...]), w_ref[...]))
        squares = jnp.sum(value * value, axis=1, keepdims=True)
        first = pl.program_id(0) == 0

        @pl.when(first)
        def _():
            out_ref[:, :cols] = raw
            out_ref[:, cols:] = jnp.broadcast_to(squares, (rows, lanes))

        @pl.when(jnp.logical_not(first))
        def _():
            out_ref[:, :cols] += raw
            out_ref[:, cols:] += jnp.broadcast_to(squares, (rows, lanes))

    by_depth = pl.BlockSpec((rows, block), lambda k: (0, k))
    return call(
        kernel,
        [x, gain, w, *parts, *waits],
        [
            by_depth,
            pl.BlockSpec((1, block), lambda k: (0, k)),
            pl.BlockSpec((block, cols), lambda k: (k, 0)),
        ]
        + [by_depth] * n
        + [ANY] * len(waits),
        [
            jax.ShapeDtypeStruct((rows, cols + lanes), F32),
            jax.ShapeDtypeStruct((rows, depth), F32),
        ],
        [pl.BlockSpec((rows, cols + lanes), lambda k: (0, 0)), by_depth],
        (depth // block,),
        [],
        (4 * rows * depth * cols, 2 * depth * cols),
        12 if n else 60,
    )


def state_rows(rows):
    blocks = -(-rows // 128)
    return blocks, rows + 8 * (-(-2 * blocks // 8))


def eye(rows):
    return lax.broadcasted_iota(jnp.int32, (rows, 128), 0) == lax.broadcasted_iota(
        jnp.int32, (rows, 128), 1
    )


def attend(parts, cosine, sine, old, keys, values, token_req, owner, group_q, waits):
    total_req, width = parts[0].shape
    tokens, head_dim = keys.shape
    rows = group_q * total_req
    chunk = math.gcd(tokens, 2048)
    n, n_old = len(parts), len(old)
    blocks, out_rows = state_rows(rows)
    score_scale = 1.0 / math.sqrt(head_dim)
    steps = tokens // chunk

    def kernel(*refs):
        part_refs, refs = refs[:n], refs[n:]
        old_refs, refs = refs[:n_old], refs[n_old:]
        cos_ref, sin_ref, owner_ref, req_ref, k_ref, v_ref, *refs = refs
        refs = refs[len(waits) :]
        state_ref, fresh_k_ref, fresh_v_ref, q_ref, q2_ref, m_ref, l_ref, acc_ref = refs
        index = pl.program_id(0)

        @pl.when(index == 0)
        def _():
            packed = tree_sum([r[...] for r in part_refs])
            scale = lax.rsqrt(packed[:, width - 1 :] / D + epsilon)
            cos, sin = cos_ref[...], sin_ref[...]

            def rotated(at):
                y = packed[:, at * head_dim : (at + 1) * head_dim] * scale
                return y * cos + pltpu.roll(y, head_dim // 2, 1) * sin

            for g in range(group_q):
                q_ref[g * total_req : (g + 1) * total_req, :] = rotated(g) * score_scale
            query = q_ref[...]
            q2_ref[...] = split_rows(query)
            fresh_k = rotated(group_q)
            fresh_v = packed[:, (group_q + 1) * head_dim : (group_q + 2) * head_dim] * scale
            fresh_k_ref[...] = fresh_k
            fresh_v_ref[...] = fresh_v
            ks = [r[...] for r in old_refs[0::2]] + [fresh_k]
            vs = [r[...] for r in old_refs[1::2]] + [fresh_v]
            scores = [
                jnp.sum(query * jnp.concatenate([k] * group_q), axis=1, keepdims=True) for k in ks
            ]
            top = functools.reduce(jnp.maximum, scores)
            weights = [jnp.exp(s - top) for s in scores]
            acc = sum(w * jnp.concatenate([v] * group_q) for w, v in zip(weights, vs))
            own = jnp.full((rows, 128), owner_ref[0], jnp.int32) == 1
            m_ref[...] = jnp.where(own, jnp.broadcast_to(top, (rows, 128)), NEG)
            l_ref[...] = jnp.where(own, jnp.broadcast_to(sum(weights), (rows, 128)), 0.0)
            acc_ref[...] = jnp.where(own, acc, 0.0)

        scores = join_rows(dot(q2_ref[...], k_ref[...], ((1,), (1,))))
        row_req = lax.rem(lax.broadcasted_iota(jnp.int32, (rows, chunk), 0), total_req)
        alive = jnp.broadcast_to(req_ref[...], (rows, chunk)) == row_req
        scores = jnp.where(alive, scores, NEG)
        old_top = m_ref[:, :1]
        top = jnp.maximum(old_top, jnp.max(scores, axis=1, keepdims=True))
        weights = jnp.where(alive, jnp.exp(scores - top), 0.0)
        factor = jnp.exp(old_top - top)
        total = l_ref[:, :1] * factor + jnp.sum(weights, axis=1, keepdims=True)
        acc = acc_ref[...] * factor + join_rows(dot(split_rows(weights), v_ref[...]))
        m_ref[...] = jnp.broadcast_to(top, (rows, 128))
        l_ref[...] = jnp.broadcast_to(total, (rows, 128))
        acc_ref[...] = acc

        @pl.when(index == steps - 1)
        def _():
            state_ref[:rows, :] = acc
            lines = []
            for column in (top, total):
                for b in range(blocks):
                    part = column[b * 128 : (b + 1) * 128]
                    lines.append(
                        jnp.sum(jnp.where(eye(part.shape[0]), part, 0.0), axis=0, keepdims=True)
                    )
            if len(lines) < out_rows - rows:
                lines.append(jnp.zeros((out_rows - rows - len(lines), 128), F32))
            state_ref[rows:, :] = jnp.concatenate(lines)

    def fixed(array):
        return pl.BlockSpec(array.shape, lambda i: (0, 0))

    fresh = jax.ShapeDtypeStruct((total_req, head_dim), F32)
    by_token = pl.BlockSpec((chunk, head_dim), lambda i: (i, 0))
    return call(
        kernel,
        [*parts, *old, cosine, sine, owner, token_req, keys, values, *waits],
        [fixed(a) for a in (*parts, *old, cosine, sine)]
        + [SMEM, pl.BlockSpec((1, chunk), lambda i: (0, i)), by_token, by_token]
        + [ANY] * len(waits),
        [jax.ShapeDtypeStruct((out_rows, 128), F32), fresh, fresh],
        [pl.BlockSpec((out_rows, 128), lambda i: (0, 0))]
        + [pl.BlockSpec((total_req, head_dim), lambda i: (0, 0))] * 2,
        (steps,),
        [
            pltpu.VMEM((rows, head_dim), F32),
            pltpu.VMEM((2 * rows, head_dim), BF16),
            pltpu.VMEM((rows, 128), F32),
            pltpu.VMEM((rows, 128), F32),
            pltpu.VMEM((rows, head_dim), F32),
        ],
        (8 * rows * tokens * head_dim, 4 * tokens * head_dim),
        8 + rows // 16,
    )


def read_state(state, rows):
    blocks, _ = state_rows(rows)
    columns = []
    for first in (rows, rows + blocks):
        pieces = []
        for b in range(blocks):
            size = min(128, rows - b * 128)
            line = jnp.broadcast_to(state[first + b : first + b + 1], (size, 128))
            pieces.append(jnp.sum(jnp.where(eye(size), line, 0.0), axis=1, keepdims=True))
        columns.append(jnp.concatenate(pieces))
    return state[:rows], columns[0], columns[1]


def output(states, w, total_req, group_q, waits):
    rows = total_req * group_q
    depth, cols = w.shape
    block = math.gcd(cols, 512)
    out_rows = state_rows(rows)[1]
    held = states[0].shape[0] // out_rows
    n = len(states)

    def kernel(*refs):
        state_refs, w_ref, (out_ref, att_ref) = refs[:n], refs[n], refs[-2:]

        @pl.when(pl.program_id(0) == 0)
        def _():
            read = [
                read_state(r[h * out_rows : (h + 1) * out_rows], rows)
                for r in state_refs
                for h in range(held)
            ]
            best = functools.reduce(jnp.maximum, [top for _, top, _ in read])
            factors = [jnp.exp(top - best) for _, top, _ in read]
            acc = sum(a * f for (a, _, _), f in zip(read, factors))
            total = sum(t * f for (_, _, t), f in zip(read, factors))
            attended = acc / total
            by_row = jnp.concatenate(
                [attended[g * total_req : (g + 1) * total_req] for g in range(group_q)], axis=1
            )
            att_ref[...] = split_rows(by_row)

        out_ref[...] = join_rows(dot(att_ref[...], w_ref[...]))

    return call(
        kernel,
        [*states, w, *waits],
        [pl.BlockSpec(s.shape, lambda c: (0, 0)) for s in states]
        + [pl.BlockSpec((depth, block), lambda c: (0, c))]
        + [ANY] * len(waits),
        [jax.ShapeDtypeStruct((total_req, cols), F32)],
        [pl.BlockSpec((total_req, block), lambda c: (0, c))],
        (cols // block,),
        [pltpu.VMEM((2 * total_req, depth), BF16)],
        (4 * total_req * depth * cols, 2 * depth * cols),
        12 + rows // 16,
    )


def unpack(pieces, spec, table, ids, shape, pair, before=()):
    n = len(pieces)
    part_pages = shape[2]

    far = not before

    def kernel(table_ref, ids_ref, *refs):
        piece_refs, rest = refs[:n], refs[n + len(before) :]
        outs, sems, held = rest[:2], rest[2], rest[3:]
        if far:
            loads = [
                pltpu.make_async_copy(p, held[0].at[c], held[1].at[c])
                for c, p in enumerate(piece_refs)
            ]
            for load in loads:
                load.start()
            piece_refs = [held[0].at[c] for c in range(n)]
        for c, (piece, (dj, dr)) in enumerate(zip(piece_refs, spec)):
            if far:
                loads[c].wait()
            for k in range(pair):
                at = table_ref[(ids_ref[1] ^ dr) * pair + k]
                request = lax.div(at, part_pages)
                page = at - request * part_pages
                for which, out in enumerate(outs):
                    pltpu.make_async_copy(
                        piece.at[which, k], out.at[request, ids_ref[0] ^ dj, page], sems.at[c]
                    ).start()
        for c, piece in enumerate(piece_refs):
            pltpu.make_async_copy(piece, piece, sems.at[c]).wait()

    result = jax.ShapeDtypeStruct(shape, BF16)
    scratch = [pltpu.SemaphoreType.DMA((n,))]
    if far:
        scratch += [pltpu.VMEM((n, *pieces[0].shape), BF16), pltpu.SemaphoreType.DMA((n,))]
    return pl.pallas_call(
        kernel,
        in_specs=[SMEM, SMEM] + [HBM if far else VMEM] * n + [ANY] * len(before),
        out_specs=[HBM, HBM],
        out_shape=[result, result],
        scratch_shapes=scratch,
        input_output_aliases={2 + n: 0, 3 + n: 1} if before else {},
        compiler_params=pltpu.CompilerParams(vmem_limit_bytes=(8 if far else 2) * 1024 * 1024),
        cost_estimate=pl.CostEstimate(flops=0, bytes_accessed=1024, transcendentals=0),
    )(table, ids, *pieces, *before)


def body(hidden, gain, w_qkv, w_out, k_pool, v_pool, block_table, lengths):
    n_req = lax.axis_size("req")
    n_pre = lax.axis_size("pre")
    req_index = lax.axis_index("req")
    pre_index = lax.axis_index("pre")
    total_req, pages_per = block_table.shape
    req_local = total_req // n_req
    part_pages = pages_per // n_pre
    pages_local, _, page_len, head_dim = k_pool.shape
    dest_count = n_req * n_pre
    pair = pages_local // dest_count
    group_q = w_out.shape[0] // head_dim
    local = req_local * part_pages
    pools = [p.reshape(pages_local, page_len, head_dim) for p in (k_pool, v_pool)]
    ids = jnp.stack([pre_index, req_index]).astype(jnp.int32)

    by_dest = (
        block_table.reshape(n_req, req_local, n_pre, part_pages)
        .transpose(2, 0, 1, 3)
        .reshape(dest_count, local)
    )
    order = jnp.arange(local, dtype=jnp.int32)
    ranks = jnp.arange(pair, dtype=jnp.int32)

    def ranked(member, value):
        before = member[:, None, :] & (order[None, :] < order[:, None])[None]
        rank = jnp.sum(before.astype(jnp.int32), axis=2)
        picked = (rank[:, None, :] == ranks[None, :, None]) & member[:, None, :]
        return jnp.sum(jnp.where(picked, value[:, None, :], 0), axis=2).reshape(-1)

    send_slot = ranked(by_dest // pages_local == req_index, by_dest % pages_local)
    my_pages = lax.dynamic_slice_in_dim(by_dest, pre_index * n_req + req_index, 1, 0)
    groups = jnp.arange(n_req, dtype=jnp.int32)[:, None]
    recv_place = ranked(
        my_pages // pages_local == groups, jnp.broadcast_to(order, (n_req, local))
    )

    slot_ids = req_index * pages_local + jnp.arange(pages_local, dtype=jnp.int32)
    flat = block_table.reshape(-1)
    place = jnp.sum(
        jnp.where(
            flat[None, :] == slot_ids[:, None],
            jnp.arange(flat.shape[0], dtype=jnp.int32)[None, :],
            0,
        ),
        axis=1,
    )
    slot_req = place // pages_per
    request_ids = jnp.arange(total_req, dtype=jnp.int32)
    length_of = jnp.sum(
        jnp.where(slot_req[:, None] == request_ids[None, :], lengths[None, :], 0), axis=1
    )
    slot_valid = length_of - (place % pages_per) * page_len
    token_req = jnp.where(
        jnp.arange(page_len, dtype=jnp.int32)[None, :] < slot_valid[:, None], slot_req[:, None], -1
    ).reshape(1, pages_local * page_len)

    half_dim = head_dim // 2
    frequency = rope_theta ** (-jnp.arange(half_dim, dtype=F32) * 2.0 / head_dim)
    positions = (lengths[None, :] + jnp.arange(STEPS, dtype=jnp.int32)[:, None]).astype(F32)
    angles = positions[:, :, None] * frequency
    cosine = jnp.concatenate([jnp.cos(angles)] * 2, -1)
    sine = jnp.concatenate([-jnp.sin(angles), jnp.sin(angles)], -1)

    by_pieces = small("req") and small("pre")
    if by_pieces:
        near = [(dj, dr) for dr in (1, 0) for dj in range(n_pre) if (dj or dr) and dr < n_req]
        far = [(dj, dr) for dj in range(n_pre) for dr in range(2, n_req)]
        counts = [(1, 1), (1, 0), (1, 0), (1, 1)]
        plan = []
        for n_far, n_near in counts:
            plan.append(far[:n_far] + near[:n_near])
            far, near = far[n_far:], near[n_near:]
        plan.append(far + near)
        spec = [piece for group in plan for piece in group] + [(0, 0)]
        packed = dict(zip(spec, pack(pools, send_slot, ids, spec, n_req, pair)))
        received = {(0, 0): packed[0, 0]}

    def send(index, terms):
        if not by_pieces:
            return
        group = plan[index]
        for (dj, dr), piece in zip(group, after([packed[p] for p in group], terms)):
            pairs = [
                (j * n_req + r, (j ^ dj) * n_req + (r ^ dr))
                for j in range(n_pre)
                for r in range(n_req)
            ]
            received[dj, dr] = lax.ppermute(piece, ("pre", "req"), pairs)

    def sent(*indices):
        return [received[p] for i in indices for p in plan[i]] if by_pieces else []

    keys = k_pool.reshape(pages_local * page_len, head_dim)
    values = v_pool.reshape(pages_local * page_len, head_dim)
    owner = (req_index == 0).astype(jnp.int32).reshape(1)
    gain_row = gain.reshape(1, -1)
    x = hidden
    parts = []
    old = []
    after_raw, after_state = [[0], [3]], [[1, 2], [4]]
    at_project, at_attend, at_output = [[], [1]], [[], [2]], [[0], [3]]
    for step in range(STEPS):
        raw, x = project(x, parts, gain_row, w_qkv, sent(*at_project[step]))
        raws = terms_over(raw, "req")
        for index in after_raw[step]:
            send(index, raws)
        state, fresh_k, fresh_v = attend(
            raws, cosine[step], sine[step], old, keys, values, token_req, owner, group_q,
            sent(*at_attend[step]),
        )
        old = old + [fresh_k, fresh_v]
        if small("req"):
            states = peers(state, "req")
        else:
            states = [lax.all_gather(state, "req", axis=0, tiled=True)]
        for index in after_state[step]:
            send(index, states)
        (partial,) = output(states, w_out, total_req, group_q, sent(*at_output[step]))
        parts = terms_over(tree_sum(terms_over(partial, "hd")), "pre")
    residual = (x + tree_sum(parts)).astype(BF16)

    shape = (req_local, n_pre, part_pages, page_len, head_dim)
    if by_pieces:
        late = spec[-4:-1]
        early = [p for p in spec if p not in late]
        outs = ()
        for group in (early, late):
            outs = unpack([received[p] for p in group], group, recv_place, ids, shape, pair, outs)
    else:
        outs = []
        for pool in pools:
            chunk = pool[send_slot].reshape(dest_count, pair, page_len, head_dim)
            chunk = lax.all_to_all(chunk, ("pre", "req"), split_axis=0, concat_axis=0, tiled=True)
            chunk = chunk.reshape(n_pre, n_req * pair, page_len, head_dim)
            placed = jnp.zeros((local, n_pre, page_len, head_dim), BF16)
            placed = placed.at[recv_place].set(chunk.transpose(1, 0, 2, 3))
            placed = placed.reshape(req_local, part_pages, n_pre, page_len, head_dim)
            outs.append(placed.transpose(0, 2, 1, 3, 4))
    outs = [o.reshape(req_local, n_pre, part_pages * page_len, head_dim) for o in outs]
    return (residual, *outs)


def solution(mesh):
    return jax.shard_map(
        body,
        mesh=mesh,
        in_specs=(
            P(None, "req"),
            P("req"),
            P("req", ("pre", "hd")),
            P(("pre", "hd"), "req"),
            P("req", ("pre", "hd"), None, None),
            P("req", ("pre", "hd"), None, None),
            P(),
            P(),
        ),
        out_specs=(P(None, "req"), P("req", "hd", "pre", None), P("req", "hd", "pre", None)),
        check_vma=False,
    )
```

```python
import functools
import math

import jax
import jax.numpy as jnp
from jax import lax
from jax.experimental import pallas as pl
from jax.experimental.pallas import tpu as pltpu
from jax.sharding import PartitionSpec as P

D = 8192
STEPS = 2

epsilon = 1e-05
rope_theta = 500000.0
NEG = -1e30
F32 = jnp.float32
BF16 = jnp.bfloat16
ANY = pl.BlockSpec(memory_space=pl.ANY)
SMEM = pl.BlockSpec(memory_space=pltpu.SMEM)
VMEM = pl.BlockSpec(memory_space=pltpu.VMEM)
HBM = pl.BlockSpec(memory_space=pltpu.HBM)


def peers(value, axis):
    n = lax.axis_size(axis)
    return [value] + [
        lax.ppermute(value, axis, [(i, i ^ s) for i in range(n)]) for s in range(1, n)
    ]


def small(axis):
    n = lax.axis_size(axis)
    return n <= 4 and n & (n - 1) == 0


def tree_sum(parts):
    while len(parts) > 1:
        parts = [parts[i] + parts[i + 1] for i in range(0, len(parts), 2)]
    return parts[0]


def terms_over(value, axis):
    return peers(value, axis) if small(axis) else [lax.psum(value, axis)]


def split_rows(value):
    high = value.astype(BF16)
    low = (value - high.astype(F32)).astype(BF16)
    return jnp.concatenate([high, low])


def join_rows(both):
    rows = both.shape[0] // 2
    return both[:rows] + both[rows:]


def dot(a, b, contract=((1,), (0,))):
    return lax.dot_general(a, b, (contract, ((), ())), preferred_element_type=F32)


def pack(pools, table, ids, spec, n_req, pair):
    n = len(spec)

    def kernel(table_ref, ids_ref, k_ref, v_ref, *refs):
        outs, (held, sems) = refs[:n], refs[n:]
        copies = []
        for c, (out, (dj, dr)) in enumerate(zip(outs, spec)):
            first = ((ids_ref[0] ^ dj) * n_req + (ids_ref[1] ^ dr)) * pair
            for k in range(pair):
                slot = table_ref[first + k]
                held[c, 0, k] = k_ref[slot]
                held[c, 1, k] = v_ref[slot]
            copies.append(pltpu.make_async_copy(held.at[c], out, sems.at[c]))
            copies[-1].start()
        for copy in copies:
            copy.wait()

    piece = (2, pair, *pools[0].shape[1:])
    return pl.pallas_call(
        kernel,
        in_specs=[SMEM, SMEM, VMEM, VMEM],
        out_specs=[HBM] * n,
        out_shape=[pltpu.HBM(piece, BF16)] * n,
        scratch_shapes=[pltpu.VMEM((n, *piece), BF16), pltpu.SemaphoreType.DMA((n,))],
        compiler_params=pltpu.CompilerParams(vmem_limit_bytes=16 * 1024 * 1024),
        cost_estimate=pl.CostEstimate(flops=0, bytes_accessed=1024, transcendentals=0),
    )(table, ids, *pools)


def after(values, others, space=HBM):
    n = len(values)
    if not others:
        return values
    shape = pltpu.HBM if space is HBM else jax.ShapeDtypeStruct
    return pl.pallas_call(
        lambda *refs: None,
        in_specs=[space] * n + [ANY] * len(others),
        out_specs=[space] * n,
        out_shape=[shape(v.shape, v.dtype) for v in values],
        input_output_aliases={i: i for i in range(n)},
        compiler_params=pltpu.CompilerParams(vmem_limit_bytes=1024 * 1024),
        cost_estimate=pl.CostEstimate(flops=0, bytes_accessed=1024, transcendentals=0),
    )(*values, *others)


def call(kernel, operands, in_specs, out_shapes, out_specs, grid, scratch, cost, vmem=12):
    return pl.pallas_call(
        kernel,
        grid=grid,
        in_specs=in_specs,
        out_specs=out_specs,
        out_shape=out_shapes,
        scratch_shapes=scratch,
        compiler_params=pltpu.CompilerParams(vmem_limit_bytes=vmem * 1024 * 1024),
        cost_estimate=pl.CostEstimate(flops=0, bytes_accessed=1024, transcendentals=0),
    )(*operands)


def project(x, parts, gain, w):
    rows, depth = x.shape
    cols = w.shape[1]
    block = math.gcd(depth, 512)
    lanes = 128
    n = len(parts)

    def kernel(*refs):
        x_ref, gain_ref, w_ref = refs[:3]
        part_refs = refs[3 : 3 + n]
        out_ref, new_ref = refs[-2:]
        value = x_ref[...].astype(F32)
        if n:
            value = value + tree_sum([r[...] for r in part_refs])
        new_ref[...] = value
        raw = join_rows(dot(split_rows(value * gain_ref[...]), w_ref[...]))
        squares = jnp.sum(value * value, axis=1, keepdims=True)
        first = pl.program_id(0) == 0

        @pl.when(first)
        def _():
            out_ref[:, :cols] = raw
            out_ref[:, cols:] = jnp.broadcast_to(squares, (rows, lanes))

        @pl.when(jnp.logical_not(first))
        def _():
            out_ref[:, :cols] += raw
            out_ref[:, cols:] += jnp.broadcast_to(squares, (rows, lanes))

    by_depth = pl.BlockSpec((rows, block), lambda k: (0, k))
    return call(
        kernel,
        [x, gain, w, *parts],
        [
            by_depth,
            pl.BlockSpec((1, block), lambda k: (0, k)),
            pl.BlockSpec((block, cols), lambda k: (k, 0)),
        ]
        + [by_depth] * n,
        [
            jax.ShapeDtypeStruct((rows, cols + lanes), F32),
            jax.ShapeDtypeStruct((rows, depth), F32),
        ],
        [pl.BlockSpec((rows, cols + lanes), lambda k: (0, 0)), by_depth],
        (depth // block,),
        [],
        (4 * rows * depth * cols, 2 * depth * cols),
        12 if n else 60,
    )


def state_rows(rows):
    blocks = -(-rows // 128)
    return blocks, rows + 8 * (-(-2 * blocks // 8))


def eye(rows):
    return lax.broadcasted_iota(jnp.int32, (rows, 128), 0) == lax.broadcasted_iota(
        jnp.int32, (rows, 128), 1
    )


def attend(parts, cosine, sine, old, keys, values, token_req, owner, group_q, waits):
    total_req, width = parts[0].shape
    tokens, head_dim = keys.shape
    rows = group_q * total_req
    chunk = math.gcd(tokens, 2048)
    n, n_old = len(parts), len(old)
    blocks, out_rows = state_rows(rows)
    score_scale = 1.0 / math.sqrt(head_dim)
    steps = tokens // chunk

    def kernel(*refs):
        part_refs, refs = refs[:n], refs[n:]
        old_refs, refs = refs[:n_old], refs[n_old:]
        cos_ref, sin_ref, owner_ref, req_ref, k_ref, v_ref, *refs = refs
        refs = refs[len(waits) :]
        state_ref, fresh_k_ref, fresh_v_ref, q_ref, q2_ref, m_ref, l_ref, acc_ref = refs
        index = pl.program_id(0)

        @pl.when(index == 0)
        def _():
            packed = tree_sum([r[...] for r in part_refs])
            scale = lax.rsqrt(packed[:, width - 1 :] / D + epsilon)
            cos, sin = cos_ref[...], sin_ref[...]

            def rotated(at):
                y = packed[:, at * head_dim : (at + 1) * head_dim] * scale
                return y * cos + pltpu.roll(y, head_dim // 2, 1) * sin

            for g in range(group_q):
                q_ref[g * total_req : (g + 1) * total_req, :] = rotated(g) * score_scale
            query = q_ref[...]
            q2_ref[...] = split_rows(query)
            fresh_k = rotated(group_q)
            fresh_v = packed[:, (group_q + 1) * head_dim : (group_q + 2) * head_dim] * scale
            fresh_k_ref[...] = fresh_k
            fresh_v_ref[...] = fresh_v
            ks = [r[...] for r in old_refs[0::2]] + [fresh_k]
            vs = [r[...] for r in old_refs[1::2]] + [fresh_v]
            scores = [
                jnp.sum(query * jnp.concatenate([k] * group_q), axis=1, keepdims=True) for k in ks
            ]
            top = functools.reduce(jnp.maximum, scores)
            weights = [jnp.exp(s - top) for s in scores]
            acc = sum(w * jnp.concatenate([v] * group_q) for w, v in zip(weights, vs))
            own = jnp.full((rows, 128), owner_ref[0], jnp.int32) == 1
            m_ref[...] = jnp.where(own, jnp.broadcast_to(top, (rows, 128)), NEG)
            l_ref[...] = jnp.where(own, jnp.broadcast_to(sum(weights), (rows, 128)), 0.0)
            acc_ref[...] = jnp.where(own, acc, 0.0)

        scores = join_rows(dot(q2_ref[...], k_ref[...], ((1,), (1,))))
        row_req = lax.rem(lax.broadcasted_iota(jnp.int32, (rows, chunk), 0), total_req)
        alive = jnp.broadcast_to(req_ref[...], (rows, chunk)) == row_req
        scores = jnp.where(alive, scores, NEG)
        old_top = m_ref[:, :1]
        top = jnp.maximum(old_top, jnp.max(scores, axis=1, keepdims=True))
        weights = jnp.where(alive, jnp.exp(scores - top), 0.0)
        factor = jnp.exp(old_top - top)
        total = l_ref[:, :1] * factor + jnp.sum(weights, axis=1, keepdims=True)
        acc = acc_ref[...] * factor + join_rows(dot(split_rows(weights), v_ref[...]))
        m_ref[...] = jnp.broadcast_to(top, (rows, 128))
        l_ref[...] = jnp.broadcast_to(total, (rows, 128))
        acc_ref[...] = acc

        @pl.when(index == steps - 1)
        def _():
            state_ref[:rows, :] = acc
            lines = []
            for column in (top, total):
                for b in range(blocks):
                    part = column[b * 128 : (b + 1) * 128]
                    lines.append(
                        jnp.sum(jnp.where(eye(part.shape[0]), part, 0.0), axis=0, keepdims=True)
                    )
            if len(lines) < out_rows - rows:
                lines.append(jnp.zeros((out_rows - rows - len(lines), 128), F32))
            state_ref[rows:, :] = jnp.concatenate(lines)

    def fixed(array):
        return pl.BlockSpec(array.shape, lambda i: (0, 0))

    fresh = jax.ShapeDtypeStruct((total_req, head_dim), F32)
    by_token = pl.BlockSpec((chunk, head_dim), lambda i: (i, 0))
    return call(
        kernel,
        [*parts, *old, cosine, sine, owner, token_req, keys, values, *waits],
        [fixed(a) for a in (*parts, *old, cosine, sine)]
        + [SMEM, pl.BlockSpec((1, chunk), lambda i: (0, i)), by_token, by_token]
        + [ANY] * len(waits),
        [jax.ShapeDtypeStruct((out_rows, 128), F32), fresh, fresh],
        [pl.BlockSpec((out_rows, 128), lambda i: (0, 0))]
        + [pl.BlockSpec((total_req, head_dim), lambda i: (0, 0))] * 2,
        (steps,),
        [
            pltpu.VMEM((rows, head_dim), F32),
            pltpu.VMEM((2 * rows, head_dim), BF16),
            pltpu.VMEM((rows, 128), F32),
            pltpu.VMEM((rows, 128), F32),
            pltpu.VMEM((rows, head_dim), F32),
        ],
        (8 * rows * tokens * head_dim, 4 * tokens * head_dim),
        8 + rows // 16,
    )


def read_state(state, rows):
    blocks, _ = state_rows(rows)
    columns = []
    for first in (rows, rows + blocks):
        pieces = []
        for b in range(blocks):
            size = min(128, rows - b * 128)
            line = jnp.broadcast_to(state[first + b : first + b + 1], (size, 128))
            pieces.append(jnp.sum(jnp.where(eye(size), line, 0.0), axis=1, keepdims=True))
        columns.append(jnp.concatenate(pieces))
    return state[:rows], columns[0], columns[1]


def output(states, w, total_req, group_q):
    rows = total_req * group_q
    depth, cols = w.shape
    block = math.gcd(cols, 512)
    out_rows = state_rows(rows)[1]
    held = states[0].shape[0] // out_rows
    n = len(states)

    def kernel(*refs):
        state_refs, w_ref, (out_ref, att_ref) = refs[:n], refs[n], refs[-2:]

        @pl.when(pl.program_id(0) == 0)
        def _():
            read = [
                read_state(r[h * out_rows : (h + 1) * out_rows], rows)
                for r in state_refs
                for h in range(held)
            ]
            best = functools.reduce(jnp.maximum, [top for _, top, _ in read])
            factors = [jnp.exp(top - best) for _, top, _ in read]
            acc = sum(a * f for (a, _, _), f in zip(read, factors))
            total = sum(t * f for (_, _, t), f in zip(read, factors))
            attended = acc / total
            by_row = jnp.concatenate(
                [attended[g * total_req : (g + 1) * total_req] for g in range(group_q)], axis=1
            )
            att_ref[...] = split_rows(by_row)

        out_ref[...] = join_rows(dot(att_ref[...], w_ref[...]))

    return call(
        kernel,
        [*states, w],
        [pl.BlockSpec(s.shape, lambda c: (0, 0)) for s in states]
        + [pl.BlockSpec((depth, block), lambda c: (0, c))],
        [jax.ShapeDtypeStruct((total_req, cols), F32)],
        [pl.BlockSpec((total_req, block), lambda c: (0, c))],
        (cols // block,),
        [pltpu.VMEM((2 * total_req, depth), BF16)],
        (4 * total_req * depth * cols, 2 * depth * cols),
        12 + rows // 16,
    )


def unpack(pieces, spec, table, ids, shape, pair, before=(), waits=()):
    n = len(pieces)
    part_pages = shape[2]

    far = not before

    def kernel(table_ref, ids_ref, *refs):
        piece_refs, rest = refs[:n], refs[n + len(before) + len(waits) :]
        outs, sems, held = rest[:2], rest[2], rest[3:]
        if far:
            loads = [
                pltpu.make_async_copy(p, held[0].at[c], held[1].at[c])
                for c, p in enumerate(piece_refs)
            ]
            for load in loads:
                load.start()
            piece_refs = [held[0].at[c] for c in range(n)]
        for c, (piece, (dj, dr)) in enumerate(zip(piece_refs, spec)):
            if far:
                loads[c].wait()
            for k in range(pair):
                at = table_ref[(ids_ref[1] ^ dr) * pair + k]
                request = lax.div(at, part_pages)
                page = at - request * part_pages
                for which, out in enumerate(outs):
                    pltpu.make_async_copy(
                        piece.at[which, k], out.at[request, ids_ref[0] ^ dj, page], sems.at[c]
                    ).start()
        for c, piece in enumerate(piece_refs):
            pltpu.make_async_copy(piece, piece, sems.at[c]).wait()

    result = jax.ShapeDtypeStruct(shape, BF16)
    scratch = [pltpu.SemaphoreType.DMA((n,))]
    if far:
        scratch += [pltpu.VMEM((n, *pieces[0].shape), BF16), pltpu.SemaphoreType.DMA((n,))]
    return pl.pallas_call(
        kernel,
        in_specs=[SMEM, SMEM] + [HBM if far else VMEM] * n + [ANY] * (len(before) + len(waits)),
        out_specs=[HBM, HBM],
        out_shape=[result, result],
        scratch_shapes=scratch,
        input_output_aliases={2 + n: 0, 3 + n: 1} if before else {},
        compiler_params=pltpu.CompilerParams(vmem_limit_bytes=(8 if far else 2) * 1024 * 1024),
        cost_estimate=pl.CostEstimate(
            flops=0, bytes_accessed=16 * 1024 * 1024 if far else 1024, transcendentals=0
        ),
    )(table, ids, *pieces, *before, *waits)


def body(hidden, gain, w_qkv, w_out, k_pool, v_pool, block_table, lengths):
    n_req = lax.axis_size("req")
    n_pre = lax.axis_size("pre")
    req_index = lax.axis_index("req")
    pre_index = lax.axis_index("pre")
    total_req, pages_per = block_table.shape
    req_local = total_req // n_req
    part_pages = pages_per // n_pre
    pages_local, _, page_len, head_dim = k_pool.shape
    dest_count = n_req * n_pre
    pair = pages_local // dest_count
    group_q = w_out.shape[0] // head_dim
    local = req_local * part_pages
    pools = [p.reshape(pages_local, page_len, head_dim) for p in (k_pool, v_pool)]
    ids = jnp.stack([pre_index, req_index]).astype(jnp.int32)

    by_dest = (
        block_table.reshape(n_req, req_local, n_pre, part_pages)
        .transpose(2, 0, 1, 3)
        .reshape(dest_count, local)
    )
    order = jnp.arange(local, dtype=jnp.int32)
    ranks = jnp.arange(pair, dtype=jnp.int32)

    def ranked(member, value):
        before = member[:, None, :] & (order[None, :] < order[:, None])[None]
        rank = jnp.sum(before.astype(jnp.int32), axis=2)
        picked = (rank[:, None, :] == ranks[None, :, None]) & member[:, None, :]
        return jnp.sum(jnp.where(picked, value[:, None, :], 0), axis=2).reshape(-1)

    send_slot = ranked(by_dest // pages_local == req_index, by_dest % pages_local)
    my_pages = lax.dynamic_slice_in_dim(by_dest, pre_index * n_req + req_index, 1, 0)
    groups = jnp.arange(n_req, dtype=jnp.int32)[:, None]
    recv_place = ranked(
        my_pages // pages_local == groups, jnp.broadcast_to(order, (n_req, local))
    )

    slot_ids = req_index * pages_local + jnp.arange(pages_local, dtype=jnp.int32)
    flat = block_table.reshape(-1)
    place = jnp.sum(
        jnp.where(
            flat[None, :] == slot_ids[:, None],
            jnp.arange(flat.shape[0], dtype=jnp.int32)[None, :],
            0,
        ),
        axis=1,
    )
    slot_req = place // pages_per
    request_ids = jnp.arange(total_req, dtype=jnp.int32)
    length_of = jnp.sum(
        jnp.where(slot_req[:, None] == request_ids[None, :], lengths[None, :], 0), axis=1
    )
    slot_valid = length_of - (place % pages_per) * page_len
    token_req = jnp.where(
        jnp.arange(page_len, dtype=jnp.int32)[None, :] < slot_valid[:, None], slot_req[:, None], -1
    ).reshape(1, pages_local * page_len)

    half_dim = head_dim // 2
    frequency = rope_theta ** (-jnp.arange(half_dim, dtype=F32) * 2.0 / head_dim)
    positions = (lengths[None, :] + jnp.arange(STEPS, dtype=jnp.int32)[:, None]).astype(F32)
    angles = positions[:, :, None] * frequency
    cosine = jnp.concatenate([jnp.cos(angles)] * 2, -1)
    sine = jnp.concatenate([-jnp.sin(angles), jnp.sin(angles)], -1)

    by_pieces = small("req") and small("pre")
    if by_pieces:
        near = [(dj, dr) for dr in (1, 0) for dj in range(n_pre) if (dj or dr) and dr < n_req]
        far = [(dj, dr) for dj in range(n_pre) for dr in range(2, n_req)]
        counts = [(1, 2), (1, 1), (2, 0), (1, 1), (2, 0)]
        plan = []
        for n_far, n_near in counts:
            plan.append(far[:n_far] + near[:n_near])
            far, near = far[n_far:], near[n_near:]
        plan.append(far + near)
        spec = [piece for group in plan for piece in group] + [(0, 0)]
        packed = dict(zip(spec, pack(pools, send_slot, ids, spec, n_req, pair)))
        received = {(0, 0): packed[0, 0]}

    def send(index, terms):
        if not by_pieces:
            return
        group = plan[index]
        pieces = [packed[p] for p in group]
        for (dj, dr), piece in zip(group, after(pieces, terms)):
            pairs = [
                (j * n_req + r, (j ^ dj) * n_req + (r ^ dr))
                for j in range(n_pre)
                for r in range(n_req)
            ]
            received[dj, dr] = lax.ppermute(piece, ("pre", "req"), pairs)

    def sent(*indices):
        return [received[p] for i in indices for p in plan[i]] if by_pieces else []

    keys = k_pool.reshape(pages_local * page_len, head_dim)
    values = v_pool.reshape(pages_local * page_len, head_dim)
    owner = (req_index == 0).astype(jnp.int32).reshape(1)
    gain_row = gain.reshape(1, -1)
    x = hidden
    parts = []
    old = []
    send(0, [])
    for step in range(STEPS):
        raw, x = project(x, parts, gain_row, w_qkv)
        if step:
            (raw,) = after([raw], sent(2), ANY)
        raws = terms_over(raw, "req")
        send((1, 3)[step], raws)
        state, fresh_k, fresh_v = attend(
            raws, cosine[step], sine[step], old, keys, values, token_req, owner, group_q,
            [] if step else sent(0),
        )
        old = old + [fresh_k, fresh_v]
        (state,) = after([state], sent((1, 3)[step]), ANY)
        if small("req"):
            states = peers(state, "req")
        else:
            states = [lax.all_gather(state, "req", axis=0, tiled=True)]
        send((2, 4)[step], states)
        (partial,) = output(states, w_out, total_req, group_q)
        parts = terms_over(tree_sum(terms_over(partial, "hd")), "pre")
    residual = (x + tree_sum(parts)).astype(BF16)
    send(5, parts + sent(4)[:1])

    shape = (req_local, n_pre, part_pages, page_len, head_dim)
    if by_pieces:
        late = plan[5]
        early = [p for p in spec if p not in late]
        outs = unpack(
            [received[p] for p in early], early, recv_place, ids, shape, pair, waits=parts
        )
        outs = unpack([received[p] for p in late], late, recv_place, ids, shape, pair, outs)
    else:
        outs = []
        for pool in pools:
            chunk = pool[send_slot].reshape(dest_count, pair, page_len, head_dim)
            chunk = lax.all_to_all(chunk, ("pre", "req"), split_axis=0, concat_axis=0, tiled=True)
            chunk = chunk.reshape(n_pre, n_req * pair, page_len, head_dim)
            placed = jnp.zeros((local, n_pre, page_len, head_dim), BF16)
            placed = placed.at[recv_place].set(chunk.transpose(1, 0, 2, 3))
            placed = placed.reshape(req_local, part_pages, n_pre, page_len, head_dim)
            outs.append(placed.transpose(0, 2, 1, 3, 4))
    outs = [o.reshape(req_local, n_pre, part_pages * page_len, head_dim) for o in outs]
    return (residual, *outs)


def solution(mesh):
    return jax.shard_map(
        body,
        mesh=mesh,
        in_specs=(
            P(None, "req"),
            P("req"),
            P("req", ("pre", "hd")),
            P(("pre", "hd"), "req"),
            P("req", ("pre", "hd"), None, None),
            P("req", ("pre", "hd"), None, None),
            P(),
            P(),
        ),
        out_specs=(P(None, "req"), P("req", "hd", "pre", None), P("req", "hd", "pre", None)),
        check_vma=False,
    )
```

```python
import functools
import math

import jax
import jax.numpy as jnp
from jax import lax
from jax.experimental import pallas as pl
from jax.experimental.pallas import tpu as pltpu
from jax.sharding import PartitionSpec as P

D = 8192
STEPS = 2

epsilon = 1e-05
rope_theta = 500000.0
NEG = -1e30
F32 = jnp.float32
BF16 = jnp.bfloat16
ANY = pl.BlockSpec(memory_space=pl.ANY)
SMEM = pl.BlockSpec(memory_space=pltpu.SMEM)
VMEM = pl.BlockSpec(memory_space=pltpu.VMEM)
HBM = pl.BlockSpec(memory_space=pltpu.HBM)


def peers(value, axis):
    n = lax.axis_size(axis)
    return [value] + [
        lax.ppermute(value, axis, [(i, i ^ s) for i in range(n)]) for s in range(1, n)
    ]


def small(axis):
    n = lax.axis_size(axis)
    return n <= 4 and n & (n - 1) == 0


def tree_sum(parts):
    while len(parts) > 1:
        parts = [parts[i] + parts[i + 1] for i in range(0, len(parts), 2)]
    return parts[0]


def terms_over(value, axis):
    return peers(value, axis) if small(axis) else [lax.psum(value, axis)]


def split_rows(value):
    high = value.astype(BF16)
    low = (value - high.astype(F32)).astype(BF16)
    return jnp.concatenate([high, low])


def join_rows(both):
    rows = both.shape[0] // 2
    return both[:rows] + both[rows:]


def dot(a, b, contract=((1,), (0,))):
    return lax.dot_general(a, b, (contract, ((), ())), preferred_element_type=F32)


def pack(pools, table, ids, spec, n_req, pair):
    n = len(spec)

    def kernel(table_ref, ids_ref, k_ref, v_ref, *refs):
        outs, (held, sems) = refs[:n], refs[n:]
        copies = []
        for c, (out, (dj, dr)) in enumerate(zip(outs, spec)):
            first = ((ids_ref[0] ^ dj) * n_req + (ids_ref[1] ^ dr)) * pair
            for k in range(pair):
                slot = table_ref[first + k]
                held[c, 0, k] = k_ref[slot]
                held[c, 1, k] = v_ref[slot]
            copies.append(pltpu.make_async_copy(held.at[c], out, sems.at[c]))
            copies[-1].start()
        for copy in copies:
            copy.wait()

    piece = (2, pair, *pools[0].shape[1:])
    return pl.pallas_call(
        kernel,
        in_specs=[SMEM, SMEM, VMEM, VMEM],
        out_specs=[HBM] * n,
        out_shape=[pltpu.HBM(piece, BF16)] * n,
        scratch_shapes=[pltpu.VMEM((n, *piece), BF16), pltpu.SemaphoreType.DMA((n,))],
        compiler_params=pltpu.CompilerParams(vmem_limit_bytes=16 * 1024 * 1024),
        cost_estimate=pl.CostEstimate(flops=0, bytes_accessed=1024, transcendentals=0),
    )(table, ids, *pools)


def after(values, others, space=HBM):
    n = len(values)
    if not others:
        return values
    shape = pltpu.HBM if space is HBM else jax.ShapeDtypeStruct
    return pl.pallas_call(
        lambda *refs: None,
        in_specs=[space] * n + [ANY] * len(others),
        out_specs=[space] * n,
        out_shape=[shape(v.shape, v.dtype) for v in values],
        input_output_aliases={i: i for i in range(n)},
        compiler_params=pltpu.CompilerParams(vmem_limit_bytes=1024 * 1024),
        cost_estimate=pl.CostEstimate(flops=0, bytes_accessed=1024, transcendentals=0),
    )(*values, *others)


def call(kernel, operands, in_specs, out_shapes, out_specs, grid, scratch, cost, vmem=12):
    return pl.pallas_call(
        kernel,
        grid=grid,
        in_specs=in_specs,
        out_specs=out_specs,
        out_shape=out_shapes,
        scratch_shapes=scratch,
        compiler_params=pltpu.CompilerParams(vmem_limit_bytes=vmem * 1024 * 1024),
        cost_estimate=pl.CostEstimate(flops=0, bytes_accessed=1024, transcendentals=0),
    )(*operands)


def project(x, parts, gain, w):
    rows, depth = x.shape
    cols = w.shape[1]
    block = math.gcd(depth, 512)
    lanes = 128
    n = len(parts)
    if not n:
        return first_project(x, gain, w)

    def kernel(*refs):
        x_ref, gain_ref, w_ref = refs[:3]
        part_refs = refs[3 : 3 + n]
        out_ref, new_ref = refs[-2:]
        value = x_ref[...].astype(F32)
        if n:
            value = value + tree_sum([r[...] for r in part_refs])
        new_ref[...] = value
        raw = join_rows(dot(split_rows(value * gain_ref[...]), w_ref[...]))
        squares = jnp.sum(value * value, axis=1, keepdims=True)
        first = pl.program_id(0) == 0

        @pl.when(first)
        def _():
            out_ref[:, :cols] = raw
            out_ref[:, cols:] = jnp.broadcast_to(squares, (rows, lanes))

        @pl.when(jnp.logical_not(first))
        def _():
            out_ref[:, :cols] += raw
            out_ref[:, cols:] += jnp.broadcast_to(squares, (rows, lanes))

    by_depth = pl.BlockSpec((rows, block), lambda k: (0, k))
    return call(
        kernel,
        [x, gain, w, *parts],
        [
            by_depth,
            pl.BlockSpec((1, block), lambda k: (0, k)),
            pl.BlockSpec((block, cols), lambda k: (k, 0)),
        ]
        + [by_depth] * n,
        [
            jax.ShapeDtypeStruct((rows, cols + lanes), F32),
            jax.ShapeDtypeStruct((rows, depth), F32),
        ],
        [pl.BlockSpec((rows, cols + lanes), lambda k: (0, 0)), by_depth],
        (depth // block,),
        [],
        (4 * rows * depth * cols, 2 * depth * cols),
        12 if n else 60,
    )


def first_project(x, gain, w):
    rows, depth = x.shape
    cols = w.shape[1]
    lanes = 128
    blocks = 8 if depth % 1024 == 0 else 1
    block = depth // blocks

    def kernel(x_ref, gain_ref, w_ref, out_ref, new_ref, held, sems):
        copies = [
            pltpu.make_async_copy(
                w_ref.at[pl.ds(b * block, block)], held.at[pl.ds(b * block, block)], sems.at[b]
            )
            for b in range(blocks)
        ]
        for copy in copies:
            copy.start()
        value = x_ref[...].astype(F32)
        new_ref[...] = value
        squares = jnp.sum(value * value, axis=1, keepdims=True)
        out_ref[:, cols:] = jnp.broadcast_to(squares, (rows, lanes))
        gained = split_rows(value * gain_ref[...])
        total = jnp.zeros((2 * rows, cols), F32)
        for b, copy in enumerate(copies):
            copy.wait()
            at = slice(b * block, (b + 1) * block)
            total = total + dot(gained[:, at], held[at, :])
        out_ref[:, :cols] = join_rows(total)

    return pl.pallas_call(
        kernel,
        in_specs=[VMEM, VMEM, ANY],
        out_specs=[VMEM, VMEM],
        out_shape=[
            jax.ShapeDtypeStruct((rows, cols + lanes), F32),
            jax.ShapeDtypeStruct((rows, depth), F32),
        ],
        scratch_shapes=[pltpu.VMEM(w.shape, w.dtype), pltpu.SemaphoreType.DMA((blocks,))],
        compiler_params=pltpu.CompilerParams(vmem_limit_bytes=60 * 1024 * 1024),
        cost_estimate=pl.CostEstimate(flops=0, bytes_accessed=1024, transcendentals=0),
    )(x, gain, w)


def state_rows(rows):
    blocks = -(-rows // 128)
    return blocks, rows + 8 * (-(-2 * blocks // 8))


def eye(rows):
    return lax.broadcasted_iota(jnp.int32, (rows, 128), 0) == lax.broadcasted_iota(
        jnp.int32, (rows, 128), 1
    )


def attend(parts, cosine, sine, old, keys, values, token_req, owner, group_q):
    total_req, width = parts[0].shape
    tokens, head_dim = keys.shape
    rows = group_q * total_req
    chunk = math.gcd(tokens, 2048)
    n, n_old = len(parts), len(old)
    blocks, out_rows = state_rows(rows)
    score_scale = 1.0 / math.sqrt(head_dim)
    steps = tokens // chunk

    def kernel(*refs):
        part_refs, refs = refs[:n], refs[n:]
        old_refs, refs = refs[:n_old], refs[n_old:]
        cos_ref, sin_ref, owner_ref, req_ref, k_ref, v_ref, *refs = refs
        state_ref, fresh_k_ref, fresh_v_ref, q_ref, q2_ref, m_ref, l_ref, acc_ref = refs
        index = pl.program_id(0)

        @pl.when(index == 0)
        def _():
            packed = tree_sum([r[...] for r in part_refs])
            scale = lax.rsqrt(packed[:, width - 1 :] / D + epsilon)
            cos, sin = cos_ref[...], sin_ref[...]

            def rotated(at):
                y = packed[:, at * head_dim : (at + 1) * head_dim] * scale
                return y * cos + pltpu.roll(y, head_dim // 2, 1) * sin

            for g in range(group_q):
                q_ref[g * total_req : (g + 1) * total_req, :] = rotated(g) * score_scale
            query = q_ref[...]
            q2_ref[...] = split_rows(query)
            fresh_k = rotated(group_q)
            fresh_v = packed[:, (group_q + 1) * head_dim : (group_q + 2) * head_dim] * scale
            fresh_k_ref[...] = fresh_k
            fresh_v_ref[...] = fresh_v
            ks = [r[...] for r in old_refs[0::2]] + [fresh_k]
            vs = [r[...] for r in old_refs[1::2]] + [fresh_v]
            scores = [
                jnp.sum(query * jnp.concatenate([k] * group_q), axis=1, keepdims=True) for k in ks
            ]
            top = functools.reduce(jnp.maximum, scores)
            weights = [jnp.exp(s - top) for s in scores]
            acc = sum(w * jnp.concatenate([v] * group_q) for w, v in zip(weights, vs))
            own = jnp.full((rows, 128), owner_ref[0], jnp.int32) == 1
            m_ref[...] = jnp.where(own, jnp.broadcast_to(top, (rows, 128)), NEG)
            l_ref[...] = jnp.where(own, jnp.broadcast_to(sum(weights), (rows, 128)), 0.0)
            acc_ref[...] = jnp.where(own, acc, 0.0)

        scores = join_rows(dot(q2_ref[...], k_ref[...], ((1,), (1,))))
        row_req = lax.rem(lax.broadcasted_iota(jnp.int32, (rows, chunk), 0), total_req)
        alive = jnp.broadcast_to(req_ref[...], (rows, chunk)) == row_req
        scores = jnp.where(alive, scores, NEG)
        old_top = m_ref[:, :1]
        top = jnp.maximum(old_top, jnp.max(scores, axis=1, keepdims=True))
        weights = jnp.where(alive, jnp.exp(scores - top), 0.0)
        factor = jnp.exp(old_top - top)
        total = l_ref[:, :1] * factor + jnp.sum(weights, axis=1, keepdims=True)
        acc = acc_ref[...] * factor + join_rows(dot(split_rows(weights), v_ref[...]))
        m_ref[...] = jnp.broadcast_to(top, (rows, 128))
        l_ref[...] = jnp.broadcast_to(total, (rows, 128))
        acc_ref[...] = acc

        @pl.when(index == steps - 1)
        def _():
            state_ref[:rows, :] = acc
            lines = []
            for column in (top, total):
                for b in range(blocks):
                    part = column[b * 128 : (b + 1) * 128]
                    lines.append(
                        jnp.sum(jnp.where(eye(part.shape[0]), part, 0.0), axis=0, keepdims=True)
                    )
            if len(lines) < out_rows - rows:
                lines.append(jnp.zeros((out_rows - rows - len(lines), 128), F32))
            state_ref[rows:, :] = jnp.concatenate(lines)

    def fixed(array):
        return pl.BlockSpec(array.shape, lambda i: (0, 0))

    fresh = jax.ShapeDtypeStruct((total_req, head_dim), F32)
    by_token = pl.BlockSpec((chunk, head_dim), lambda i: (i, 0))
    return call(
        kernel,
        [*parts, *old, cosine, sine, owner, token_req, keys, values],
        [fixed(a) for a in (*parts, *old, cosine, sine)]
        + [SMEM, pl.BlockSpec((1, chunk), lambda i: (0, i)), by_token, by_token],
        [jax.ShapeDtypeStruct((out_rows, 128), F32), fresh, fresh],
        [pl.BlockSpec((out_rows, 128), lambda i: (0, 0))]
        + [pl.BlockSpec((total_req, head_dim), lambda i: (0, 0))] * 2,
        (steps,),
        [
            pltpu.VMEM((rows, head_dim), F32),
            pltpu.VMEM((2 * rows, head_dim), BF16),
            pltpu.VMEM((rows, 128), F32),
            pltpu.VMEM((rows, 128), F32),
            pltpu.VMEM((rows, head_dim), F32),
        ],
        (8 * rows * tokens * head_dim, 4 * tokens * head_dim),
        8 + rows // 16,
    )


def read_state(state, rows):
    blocks, _ = state_rows(rows)
    columns = []
    for first in (rows, rows + blocks):
        pieces = []
        for b in range(blocks):
            size = min(128, rows - b * 128)
            line = jnp.broadcast_to(state[first + b : first + b + 1], (size, 128))
            pieces.append(jnp.sum(jnp.where(eye(size), line, 0.0), axis=1, keepdims=True))
        columns.append(jnp.concatenate(pieces))
    return state[:rows], columns[0], columns[1]


def output(states, w, total_req, group_q):
    rows = total_req * group_q
    depth, cols = w.shape
    block = math.gcd(cols, 512)
    out_rows = state_rows(rows)[1]
    held = states[0].shape[0] // out_rows
    n = len(states)

    def kernel(*refs):
        state_refs, w_ref, (out_ref, att_ref) = refs[:n], refs[n], refs[-2:]

        @pl.when(pl.program_id(0) == 0)
        def _():
            read = [
                read_state(r[h * out_rows : (h + 1) * out_rows], rows)
                for r in state_refs
                for h in range(held)
            ]
            best = functools.reduce(jnp.maximum, [top for _, top, _ in read])
            factors = [jnp.exp(top - best) for _, top, _ in read]
            acc = sum(a * f for (a, _, _), f in zip(read, factors))
            total = sum(t * f for (_, _, t), f in zip(read, factors))
            attended = acc / total
            by_row = jnp.concatenate(
                [attended[g * total_req : (g + 1) * total_req] for g in range(group_q)], axis=1
            )
            att_ref[...] = split_rows(by_row)

        out_ref[...] = join_rows(dot(att_ref[...], w_ref[...]))

    return call(
        kernel,
        [*states, w],
        [pl.BlockSpec(s.shape, lambda c: (0, 0)) for s in states]
        + [pl.BlockSpec((depth, block), lambda c: (0, c))],
        [jax.ShapeDtypeStruct((total_req, cols), F32)],
        [pl.BlockSpec((total_req, block), lambda c: (0, c))],
        (cols // block,),
        [pltpu.VMEM((2 * total_req, depth), BF16)],
        (4 * total_req * depth * cols, 2 * depth * cols),
        12 + rows // 16,
    )


def unpack(pieces, spec, table, ids, shape, pair, before=(), waits=()):
    n = len(pieces)
    part_pages = shape[2]

    far = not before

    def kernel(table_ref, ids_ref, *refs):
        piece_refs, rest = refs[:n], refs[n + len(before) + len(waits) :]
        outs, sems, held = rest[:2], rest[2], rest[3:]
        if far:
            loads = [
                pltpu.make_async_copy(p, held[0].at[c], held[1].at[c])
                for c, p in enumerate(piece_refs)
            ]
            for load in loads:
                load.start()
            piece_refs = [held[0].at[c] for c in range(n)]
        for c, (piece, (dj, dr)) in enumerate(zip(piece_refs, spec)):
            if far:
                loads[c].wait()
            for k in range(pair):
                at = table_ref[(ids_ref[1] ^ dr) * pair + k]
                request = lax.div(at, part_pages)
                page = at - request * part_pages
                for which, out in enumerate(outs):
                    pltpu.make_async_copy(
                        piece.at[which, k], out.at[request, ids_ref[0] ^ dj, page], sems.at[c]
                    ).start()
        for c, piece in enumerate(piece_refs):
            pltpu.make_async_copy(piece, piece, sems.at[c]).wait()

    result = jax.ShapeDtypeStruct(shape, BF16)
    scratch = [pltpu.SemaphoreType.DMA((n,))]
    if far:
        scratch += [pltpu.VMEM((n, *pieces[0].shape), BF16), pltpu.SemaphoreType.DMA((n,))]
    return pl.pallas_call(
        kernel,
        in_specs=[SMEM, SMEM] + [HBM if far else VMEM] * n + [ANY] * (len(before) + len(waits)),
        out_specs=[HBM, HBM],
        out_shape=[result, result],
        scratch_shapes=scratch,
        input_output_aliases={2 + n: 0, 3 + n: 1} if before else {},
        compiler_params=pltpu.CompilerParams(vmem_limit_bytes=(8 if far else 2) * 1024 * 1024),
        cost_estimate=pl.CostEstimate(
            flops=0, bytes_accessed=16 * 1024 * 1024 if far else 1024, transcendentals=0
        ),
    )(table, ids, *pieces, *before, *waits)


def body(hidden, gain, w_qkv, w_out, k_pool, v_pool, block_table, lengths):
    n_req = lax.axis_size("req")
    n_pre = lax.axis_size("pre")
    req_index = lax.axis_index("req")
    pre_index = lax.axis_index("pre")
    total_req, pages_per = block_table.shape
    req_local = total_req // n_req
    part_pages = pages_per // n_pre
    pages_local, _, page_len, head_dim = k_pool.shape
    dest_count = n_req * n_pre
    pair = pages_local // dest_count
    group_q = w_out.shape[0] // head_dim
    local = req_local * part_pages
    pools = [p.reshape(pages_local, page_len, head_dim) for p in (k_pool, v_pool)]
    ids = jnp.stack([pre_index, req_index]).astype(jnp.int32)

    by_dest = (
        block_table.reshape(n_req, req_local, n_pre, part_pages)
        .transpose(2, 0, 1, 3)
        .reshape(dest_count, local)
    )
    order = jnp.arange(local, dtype=jnp.int32)
    ranks = jnp.arange(pair, dtype=jnp.int32)

    def ranked(member, value):
        before = member[:, None, :] & (order[None, :] < order[:, None])[None]
        rank = jnp.sum(before.astype(jnp.int32), axis=2)
        picked = (rank[:, None, :] == ranks[None, :, None]) & member[:, None, :]
        return jnp.sum(jnp.where(picked, value[:, None, :], 0), axis=2).reshape(-1)

    send_slot = ranked(by_dest // pages_local == req_index, by_dest % pages_local)
    my_pages = lax.dynamic_slice_in_dim(by_dest, pre_index * n_req + req_index, 1, 0)
    groups = jnp.arange(n_req, dtype=jnp.int32)[:, None]
    recv_place = ranked(
        my_pages // pages_local == groups, jnp.broadcast_to(order, (n_req, local))
    )

    slot_ids = req_index * pages_local + jnp.arange(pages_local, dtype=jnp.int32)
    flat = block_table.reshape(-1)
    place = jnp.sum(
        jnp.where(
            flat[None, :] == slot_ids[:, None],
            jnp.arange(flat.shape[0], dtype=jnp.int32)[None, :],
            0,
        ),
        axis=1,
    )
    slot_req = place // pages_per
    request_ids = jnp.arange(total_req, dtype=jnp.int32)
    length_of = jnp.sum(
        jnp.where(slot_req[:, None] == request_ids[None, :], lengths[None, :], 0), axis=1
    )
    slot_valid = length_of - (place % pages_per) * page_len
    token_req = jnp.where(
        jnp.arange(page_len, dtype=jnp.int32)[None, :] < slot_valid[:, None], slot_req[:, None], -1
    ).reshape(1, pages_local * page_len)

    half_dim = head_dim // 2
    frequency = rope_theta ** (-jnp.arange(half_dim, dtype=F32) * 2.0 / head_dim)
    positions = (lengths[None, :] + jnp.arange(STEPS, dtype=jnp.int32)[:, None]).astype(F32)
    angles = positions[:, :, None] * frequency
    cosine = jnp.concatenate([jnp.cos(angles)] * 2, -1)
    sine = jnp.concatenate([-jnp.sin(angles), jnp.sin(angles)], -1)

    by_pieces = small("req") and small("pre")
    if by_pieces:
        near = [
            (dj ^ (dr == 0), dr)
            for dj in range(n_pre)
            for dr in (1, 0)
            if (dr or dj ^ 1) and dr < n_req
        ]
        far = [(dj, dr) for dj in range(n_pre) for dr in range(2, n_req)]
        counts = [(1, 2), (2, 0), (1, 2), (2, 2)]
        plan = []
        for n_far, n_near in counts:
            plan.append(far[:n_far] + near[:n_near])
            far, near = far[n_far:], near[n_near:]
        plan.append(near + far)
        spec = [piece for group in plan for piece in group] + [(0, 0)]
        packed = dict(zip(spec, pack(pools, send_slot, ids, spec, n_req, pair)))
        received = {(0, 0): packed[0, 0]}

    def send(index, terms):
        if not by_pieces:
            return
        group = plan[index]
        pieces = [packed[p] for p in group]
        for (dj, dr), piece in zip(group, after(pieces, terms)):
            pairs = [
                (j * n_req + r, (j ^ dj) * n_req + (r ^ dr))
                for j in range(n_pre)
                for r in range(n_req)
            ]
            received[dj, dr] = lax.ppermute(piece, ("pre", "req"), pairs)

    def sent(*indices):
        return [received[p] for i in indices for p in plan[i]] if by_pieces else []

    keys = k_pool.reshape(pages_local * page_len, head_dim)
    values = v_pool.reshape(pages_local * page_len, head_dim)
    owner = (req_index == 0).astype(jnp.int32).reshape(1)
    gain_row = gain.reshape(1, -1)
    x = hidden
    parts = []
    old = []
    for step in range(STEPS):
        raw, x = project(x, parts, gain_row, w_qkv)
        if step:
            (raw,) = after([raw], sent(1), ANY)
        raws = terms_over(raw, "req")
        send((0, 2)[step], raws)
        state, fresh_k, fresh_v = attend(
            raws, cosine[step], sine[step], old, keys, values, token_req, owner, group_q
        )
        old = old + [fresh_k, fresh_v]
        (state,) = after([state], sent((0, 2)[step]), ANY)
        if small("req"):
            states = peers(state, "req")
        else:
            states = [lax.all_gather(state, "req", axis=0, tiled=True)]
        send((1, 3)[step], states)
        (partial,) = output(states, w_out, total_req, group_q)
        parts = terms_over(tree_sum(terms_over(partial, "hd")), "pre")
    residual = (x + tree_sum(parts)).astype(BF16)
    send(4, parts + sent(3)[:1])

    shape = (req_local, n_pre, part_pages, page_len, head_dim)
    if by_pieces:
        late = plan[4]
        early = [p for p in spec if p not in late]
        outs = unpack(
            [received[p] for p in early], early, recv_place, ids, shape, pair, waits=parts
        )
        outs = unpack([received[p] for p in late], late, recv_place, ids, shape, pair, outs)
    else:
        outs = []
        for pool in pools:
            chunk = pool[send_slot].reshape(dest_count, pair, page_len, head_dim)
            chunk = lax.all_to_all(chunk, ("pre", "req"), split_axis=0, concat_axis=0, tiled=True)
            chunk = chunk.reshape(n_pre, n_req * pair, page_len, head_dim)
            placed = jnp.zeros((local, n_pre, page_len, head_dim), BF16)
            placed = placed.at[recv_place].set(chunk.transpose(1, 0, 2, 3))
            placed = placed.reshape(req_local, part_pages, n_pre, page_len, head_dim)
            outs.append(placed.transpose(0, 2, 1, 3, 4))
    outs = [o.reshape(req_local, n_pre, part_pages * page_len, head_dim) for o in outs]
    return (residual, *outs)


def solution(mesh):
    return jax.shard_map(
        body,
        mesh=mesh,
        in_specs=(
            P(None, "req"),
            P("req"),
            P("req", ("pre", "hd")),
            P(("pre", "hd"), "req"),
            P("req", ("pre", "hd"), None, None),
            P("req", ("pre", "hd"), None, None),
            P(),
            P(),
        ),
        out_specs=(P(None, "req"), P("req", "hd", "pre", None), P("req", "hd", "pre", None)),
        check_vma=False,
    )
```
